32 devices in a mesh: tile: 8 (over z, y), vec: 4 (over x, core).
Axes of the slice: x: 2, y: 2, z: 4, core: 2. Of those that a mesh axis runs over, the one named last changes fastest.
Arguments:
- vectors: float32 [64, 16, 32, 128], P('vec', 'tile'), may hold values from -6 to 6
- previous: float32 [64, 16, 32, 128], P('vec', 'tile'), may hold values from -3 to 3
- intensity: float32 [16, 32, 128], P('tile'), may hold values from 0 to 2
- counts: int32 [8], P('tile'), may hold values from 0 to 8192
- coef_x: bfloat16 [3, 64, 64], replicated, may hold values from -0.4375 to 0.4375
- coef_p: bfloat16 [2, 64, 64], replicated, may hold values from -0.5 to 0.5
Outputs:
- x_next: float32 [64, 16, 32, 128], P('vec', 'tile')
- p_next: float32 [64, 16, 32, 128], P('vec', 'tile')
- residual_image: float32 [64, 16, 32, 128], P('vec', 'tile')
- gram_s: float32 [3, 64, 3, 64], P(None, 'vec')
- gram_a: float32 [3, 64, 3, 64], P(None, 'vec')
The draws below stay inside these ranges and needn't reach their ends.
All inputs are finite; a program needn't handle non-finite values.
Results may differ from the reference program's by a relative error of at most 0.0029.
Values may be sent and summed in bfloat16 or wider, within the bound.
A program may use at most 64 MiB of HBM per device.

```python
import math
import jax
import jax.numpy as jnp
from jax import lax

K = 64
CX = 2
CY = 32
CZ = 128
TILES = 8
NX = 16


def grid_coords():
    xs = jnp.arange(NX, dtype=jnp.int32)[:, None, None]
    ys = jnp.arange(CY, dtype=jnp.int32)[None, :, None]
    zs = jnp.arange(CZ, dtype=jnp.int32)[None, None, :]
    parity = ((xs + ys + zs) % 2).astype(jnp.float32)
    return (xs.astype(jnp.float32), ys.astype(jnp.float32), zs.astype(jnp.float32), 1.0 - 2.0 * parity)


def one_mode(key, count):
    xs, ys, zs, parity = grid_coords()
    kfx, kfy, kfz, kph = jax.random.split(key, 4)
    freq_x = jax.random.randint(kfx, (count, 1, 1, 1), 0, 3).astype(jnp.float32)
    freq_y = jax.random.randint(kfy, (count, 1, 1, 1), 0, 2).astype(jnp.float32)
    freq_z = jax.random.randint(kfz, (count, 1, 1, 1), 0, 2).astype(jnp.float32)
    phase = jax.random.uniform(kph, (count, 1, 1, 1), jnp.float32, 0.0, 2.0 * math.pi)
    angle = 2.0 * math.pi * (freq_x * xs[None] / NX + freq_y * ys[None] / CY + freq_z * zs[None] / CZ) + phase
    return jnp.cos(angle)


def cosine_modes(key, count):
    first_key, second_key = jax.random.split(key)
    return one_mode(first_key, count) + one_mode(second_key, count)


def build_columns(key, common, noise, common_share):
    share_key, split_key, smooth_key, rough_key = jax.random.split(key, 4)
    parity = grid_coords()[3]
    smooth = math.sqrt(1.0 - common_share) * cosine_modes(smooth_key, K) + math.sqrt(common_share) * common[None]
    alternating = cosine_modes(rough_key, K) * parity[None]
    noise_share = jax.random.uniform(share_key, (K, 1, 1, 1), jnp.float32, 0.25, 0.5)
    split = jax.random.uniform(split_key, (K, 1, 1, 1), jnp.float32, 0.0, 1.0)
    smooth_weight = jnp.sqrt((1.0 - noise_share) * split)
    rough_weight = jnp.sqrt((1.0 - noise_share) * (1.0 - split))
    return smooth_weight * smooth + rough_weight * alternating + jnp.sqrt(noise_share) * noise


def draw_vectors(key, part):
    common = cosine_modes(key, 1)[0]
    key = jax.random.fold_in(key, 11)
    mix_key, noise_key = jax.random.split(key, 2)
    noise = jax.random.normal(noise_key, (K, NX, CY, CZ), jnp.float32)
    combined = build_columns(mix_key, common, noise, 0.2)
    return jnp.clip(combined, -6.0, 6.0)


def draw_previous(key, part):
    common = cosine_modes(key, 1)[0]
    key = jax.random.fold_in(key, 12)
    mix_key, noise_key = jax.random.split(key, 2)
    noise = jax.random.normal(noise_key, (K, NX, CY, CZ), jnp.float32)
    combined = build_columns(mix_key, common, noise, 0.2)
    return jnp.clip(0.5 * combined, -3.0, 3.0)


def plant(result, own_key, least, top_value):
    extent = result.shape
    spot = [jax.random.randint(jax.random.fold_in(own_key, axis), (), 0, extent[axis]) for axis in range(len(extent))]
    result = result.at[tuple(spot)].set(least)
    longest = extent.index(max(extent))
    spot[longest] = (spot[longest] + 1) % extent[longest]
    return result.at[tuple(spot)].set(top_value)


def level_of(stream_key, dims, pieces, low, largest):
    level, own = 1.0, jax.random.fold_in(stream_key, 6)
    for position, blocks in pieces:
        heights = jnp.exp(jax.random.uniform(jax.random.fold_in(own, position), (blocks,), jnp.float32, low / len(pieces), largest / len(pieces)))
        level = level * jnp.repeat(heights, dims[position] // blocks).reshape([-1 if axis == position else 1 for axis in range(len(dims))])
    return level


def centred(rng, dims, spread, most, kind=jnp.bfloat16):
    drawn = jax.random.normal(rng, dims, jnp.float32) * spread
    return jnp.minimum(jnp.maximum(drawn, -most), most).astype(kind)


def setup_inputs(seed: int = 0) -> dict:
    seeds = jax.random.split(jax.random.key(seed), 7)
    vectors = draw_vectors(jax.random.fold_in(seeds[6], 71), 0)
    previous = draw_previous(jax.random.fold_in(seeds[6], 71), 0)
    intensity = jnp.clip(2.0 * jax.random.uniform(seeds[2], (NX, CY, CZ), jnp.float32) ** level_of(seeds[2], (NX, CY, CZ), ((0, 8),), -0.2, 0.2), 0.0, 2.0)
    counts = plant(jax.random.randint(seeds[3], (TILES,), 0, CX * CY * CZ + 1), jax.random.fold_in(seeds[3], 1), 0, CX * CY * CZ).astype(jnp.int32)
    coef_x = centred(seeds[4], (3, K, K), (3 * K) ** -0.5, 0.4375)
    coef_p = centred(seeds[5], (2, K, K), (2 * K) ** -0.5, 0.5)
    return {"vectors": vectors, "previous": previous, "intensity": intensity, "counts": counts, "coef_x": coef_x, "coef_p": coef_p}


offsets = ((1, 0, 0), (-1, 0, 0), (0, 1, 0), (0, -1, 0), (0, 0, 1), (0, 0, -1))

def pick(padded, offset, shape):
    dx, dy, dz = offset
    return padded[..., 1 + dx:1 + dx + shape[0], 1 + dy:1 + dy + shape[1], 1 + dz:1 + dz + shape[2]]

def graph(image_pad, weight_pad, shape):
    centre = pick(image_pad, (0, 0, 0), shape)
    gcentre = pick(weight_pad, (0, 0, 0), shape)
    weights = [jnp.exp(-(centre - pick(image_pad, o, shape)) ** 2) * gcentre * pick(weight_pad, o, shape) for o in offsets]
    degree = weights[0]
    for w in weights[1:]:
        degree = degree + w
    return (weights, lax.rsqrt(degree))

def apply_op(field, weights, inv, pad_fn, shape):
    padded = pad_fn(field * inv)
    total = weights[0] * pick(padded, offsets[0], shape)
    for w, o in zip(weights[1:], offsets[1:]):
        total = total + w * pick(padded, o, shape)
    return field - inv * total

def reference(vectors, previous, intensity, counts, coef_x, coef_p):
    shape = (NX, CY, CZ)
    xs = jnp.arange(NX, dtype=jnp.int32)
    ys = jnp.arange(CY, dtype=jnp.int32)
    zs = jnp.arange(CZ, dtype=jnp.int32)
    lin = ((xs % CX)[:, None, None] * CY + ys[None, :, None]) * CZ + zs[None, None, :]
    limit = counts[xs // CX][:, None, None]
    gvals = jnp.where(lin < limit, 1.0, 0.0).astype(jnp.float32) * 0.9 + 0.1
    image_pad = jnp.pad(intensity, 1)
    weight_pad = jnp.pad(gvals, 1)
    weights, inv = graph(image_pad, weight_pad, shape)

    def pad_fn(u):
        return jnp.pad(u, ((0, 0), (1, 1), (1, 1), (1, 1)))
    ax_img = apply_op(vectors, weights, inv, pad_fn, shape)
    ap_img = apply_op(previous, weights, inv, pad_fn, shape)
    num = lax.optimization_barrier(jnp.sum(vectors * ax_img, axis=(1, 2, 3)))
    den = lax.optimization_barrier(jnp.sum(vectors * vectors, axis=(1, 2, 3)))
    lam = num / den
    resid = ax_img - lam[:, None, None, None] * vectors
    ar_img = apply_op(resid, weights, inv, pad_fn, shape)
    nvox = NX * CY * CZ
    basis = jnp.stack([vectors, resid, previous]).astype(jnp.bfloat16).reshape(3, K, nvox).astype(jnp.float32)
    images = jnp.stack([ax_img, ar_img, ap_img]).astype(jnp.bfloat16).reshape(3, K, nvox).astype(jnp.float32)
    hi = lax.Precision.HIGHEST
    gram_s = jnp.einsum('aiv,bjv->aibj', basis, basis, precision=hi) / nvox
    gram_a = jnp.einsum('aiv,bjv->aibj', images, basis, precision=hi) / nvox
    x_next = jnp.einsum('aiv,aij->jv', basis, coef_x.astype(jnp.float32), precision=hi)
    p_next = jnp.einsum('aiv,aij->jv', basis[1:], coef_p.astype(jnp.float32), precision=hi)
    return (x_next.reshape(K, NX, CY, CZ), p_next.reshape(K, NX, CY, CZ), ar_img, gram_s, gram_a)
```

```python
import functools

import jax
import jax.numpy as jnp
from jax import lax
from jax.experimental import pallas as pl
from jax.experimental.pallas import tpu as pltpu
from jax.sharding import PartitionSpec as P

MESH = pl.DeviceIdType.MESH
F32 = jnp.float32
BF16 = jnp.bfloat16
Q = 6
CH = 1024


def kernel(
    T, nc, cy, cz, nvox,
    x_ref, p_ref, int_ref, cnt_ref, cfx_ref, cfp_ref,
    xo_ref, po_ref, ar_ref, g_ref,
    igb, igh, hb, hh, coef, W, L, axf, rf, lbuf, lamb,
    gpart, grs, gout,
    ig_s, ig_r, h_s, h_r, w_s, w_r, lam_s, lam_r, rs_s, rs_r, ag_s, ag_r,
):
    t = lax.axis_index("tile")
    v = lax.axis_index("vec")
    sib = v + 1 - 2 * (v % 2)
    across = (v + 2) % 4
    diag = (sib + 2) % 4
    tl = (t + T - 1) % T
    tr = (t + 1) % T
    rows = 2 * cy
    nl = rows * cz

    def rc(src, dst, ss, rs, tile, vec):
        return pltpu.make_async_remote_copy(
            src_ref=src, dst_ref=dst, send_sem=ss, recv_sem=rs,
            device_id={"tile": tile, "vec": vec}, device_id_type=MESH)

    barrier = pltpu.get_barrier_semaphore()
    for d in range(1, T):
        pl.semaphore_signal(barrier, inc=1, device_id={"tile": (t + d) % T, "vec": v}, device_id_type=MESH)
    pl.semaphore_signal(barrier, inc=1, device_id={"tile": t, "vec": sib}, device_id_type=MESH)
    pl.semaphore_signal(barrier, inc=1, device_id={"tile": t, "vec": across}, device_id_type=MESH)

    yy = lax.broadcasted_iota(jnp.int32, (cy, cz), 0)
    zz = lax.broadcasted_iota(jnp.int32, (cy, cz), 1)
    cnt = cnt_ref[0]
    for p in range(2):
        fg = jnp.where((p * cy + yy) * cz + zz < cnt, 1.0, 0.0).astype(F32)
        igb[p, 0] = int_ref[p]
        igb[p, 1] = fg * 0.9 + 0.1

    def to_halo(f, src):
        @pl.loop(0, nc)
        def _(c):
            for p in range(2):
                hb[f, p, c] = src[pl.ds(c * rows + p * cy, cy), :].astype(BF16)

    def spread(src, dsts):
        for r in range(rows):
            val = src[pl.ds(r, nc, stride=rows), :].astype(BF16)
            for dst in dsts:
                dst[:, r * cz:(r + 1) * cz] = val

    to_halo(0, x_ref)
    spread(x_ref, (W.at[0, v], L.at[0]))
    spread(p_ref, (W.at[1, v], L.at[2]))
    to_halo(1, p_ref)

    @pl.when(t == 0)
    def _():
        hh[0, 0] = jnp.zeros((nc, cy, cz), BF16)
        hh[1, 0] = jnp.zeros((nc, cy, cz), BF16)
        hh[2, 0] = jnp.zeros((nc, cy, cz), BF16)
        igh[0] = jnp.zeros((2, 2, cy, cz), F32)

    @pl.when(t == T - 1)
    def _():
        hh[0, 1] = jnp.zeros((nc, cy, cz), BF16)
        hh[1, 1] = jnp.zeros((nc, cy, cz), BF16)
        hh[2, 1] = jnp.zeros((nc, cy, cz), BF16)
        igh[1] = jnp.zeros((2, 2, cy, cz), F32)

    pl.semaphore_wait(barrier, T + 1)

    def ig_left():
        return rc(igb, igh.at[1], ig_s.at[0], ig_r.at[1], tl, v)

    def ig_right():
        return rc(igb, igh.at[0], ig_s.at[1], ig_r.at[0], tr, v)

    def h_left(f):
        return rc(hb.at[f, 0], hh.at[f, 1], h_s.at[f, 0], h_r.at[f, 1], tl, v)

    def h_right(f):
        return rc(hb.at[f, 1], hh.at[f, 0], h_s.at[f, 1], h_r.at[f, 0], tr, v)

    def both(left, right, what):
        @pl.when(t > 0)
        def _():
            c = right() if what == "wait_recv" else left()
            getattr(c, what)()

        @pl.when(t < T - 1)
        def _():
            c = left() if what == "wait_recv" else right()
            getattr(c, what)()

    def halo(f, what):
        both(lambda: h_left(f), lambda: h_right(f), what)

    def to_sib(f):
        return rc(W.at[f, v], W.at[f, v], w_s.at[f, 0], w_r.at[f, 0], t, sib)

    def to_across(f):
        return rc(W.at[f, v], W.at[f, v], w_s.at[f, 1], w_r.at[f, 1], t, across)

    def relay(f):
        return rc(W.at[f, across], W.at[f, across], w_s.at[f, 2], w_r.at[f, 2], t, sib)

    both(ig_left, ig_right, "start")
    halo(0, "start")
    to_across(0).start()
    to_across(1).start()
    to_sib(0).start()
    to_sib(1).start()
    halo(1, "start")

    pick = jnp.where(
        lax.broadcasted_iota(jnp.int32, (nc, 4 * nc), 1) == v * nc + lax.broadcasted_iota(jnp.int32, (nc, 4 * nc), 0),
        1.0, 0.0).astype(BF16)

    def own_t(m):
        return lax.dot_general(pick, m, (((1,), (1,)), ((), ())), preferred_element_type=F32)

    zero = jnp.zeros((nc, 4 * nc), F32)
    ct_x = jnp.concatenate([own_t(cfx_ref[0]), zero], axis=0).astype(BF16)
    ct_r = jnp.concatenate([own_t(cfx_ref[1]), own_t(cfp_ref[0])], axis=0).astype(BF16)
    ct_p = jnp.concatenate([own_t(cfx_ref[2]), own_t(cfp_ref[1])], axis=0).astype(BF16)

    both(ig_left, ig_right, "wait_recv")
    im = [igh[0, 0, 0], igh[0, 1, 0], igb[0, 0], igb[1, 0], igh[1, 0, 0], igh[1, 1, 0]]
    gg = [igh[0, 0, 1], igh[0, 1, 1], igb[0, 1], igb[1, 1], igh[1, 0, 1], igh[1, 1, 1]]

    def up(a, axis):
        return pltpu.roll(a, a.shape[axis] - 1, axis)

    def down(a, axis):
        return pltpu.roll(a, 1, axis)

    wx = [jnp.exp(-((im[k] - im[k + 1]) ** 2)) * gg[k] * gg[k + 1] for k in range(5)]
    wx[1] = jnp.where(t > 0, wx[1], 0.0)
    wx[3] = jnp.where(t < T - 1, wx[3], 0.0)
    wx[0] = jnp.where(t > 0, wx[0], 0.0)
    wx[4] = jnp.where(t < T - 1, wx[4], 0.0)
    inv, wys, wzs = {}, {}, {}
    for k in range(1, 5):
        wy = jnp.where(yy < cy - 1, jnp.exp(-((im[k] - up(im[k], 0)) ** 2)) * gg[k] * up(gg[k], 0), 0.0)
        wz = jnp.where(zz < cz - 1, jnp.exp(-((im[k] - up(im[k], 1)) ** 2)) * gg[k] * up(gg[k], 1), 0.0)
        deg = wx[k] + wx[k - 1] + wy + down(wy, 0) + wz + down(wz, 1)
        inv[k] = lax.rsqrt(deg)
        wys[k], wzs[k] = wy, wz
    cm = jnp.where(t > 0, inv[1] * wx[1] * inv[2], 0.0)
    c0 = inv[2] * wx[2] * inv[3]
    cp = jnp.where(t < T - 1, inv[3] * wx[3] * inv[4], 0.0)
    coef[0, 0] = cm
    coef[0, 1] = c0
    coef[0, 2] = cp
    for p in range(2):
        k = p + 2
        cyu = inv[k] * wys[k] * up(inv[k], 0)
        czu = inv[k] * wzs[k] * up(inv[k], 1)
        coef[1, p] = cyu
        coef[2, p] = down(cyu, 0)
        coef[3, p] = czu
        coef[4, p] = down(czu, 1)

    def stencil(src, c, f):
        fs = [src[pl.ds(c * rows, cy), :], src[pl.ds(c * rows + cy, cy), :]]
        out = []
        for p in range(2):
            a = fs[p]
            s = coef[1, p] * up(a, 0) + coef[2, p] * down(a, 0)
            s = s + coef[3, p] * up(a, 1) + coef[4, p] * down(a, 1)
            s = s + coef[0, 1] * fs[1 - p]
            s = s + coef[0, 2 * p] * hh[f, p, c].astype(F32)
            out.append(a - s)
        return fs, out

    halo(0, "wait_recv")
    lbuf[...] = jnp.zeros_like(lbuf)

    @pl.loop(0, nc)
    def _(c):
        fs, out = stencil(x_ref, c, 0)
        axf[pl.ds(c * rows, cy), :] = out[0]
        axf[pl.ds(c * rows + cy, cy), :] = out[1]
        num = fs[0] * out[0] + fs[1] * out[1]
        den = fs[0] * fs[0] + fs[1] * fs[1]
        lbuf[pl.ds(c, 1), :] = jnp.sum(num, axis=0, keepdims=True)
        lbuf[pl.ds(nc + c, 1), :] = jnp.sum(den, axis=0, keepdims=True)

    lamb[0] = lax.dot_general(
        jnp.ones((8, cz), F32), lbuf[...], (((1,), (1,)), ((), ())),
        precision=lax.Precision.HIGHEST, preferred_element_type=F32)

    def lam_copy(d):
        return rc(lamb.at[0], lamb.at[d], lam_s.at[d], lam_r.at[d], (t + d) % T, v)

    for d in range(1, T):
        lam_copy(d).start()
    spread(axf, (L.at[3],))
    for d in range(1, T):
        lam_copy(d).wait_recv()
    tot = lamb[0]
    for d in range(1, T):
        tot = tot + lamb[d]

    for c in range(nc):
        lam = tot[0:1, c:c + 1] / tot[0:1, nc + c:nc + c + 1]
        rr = axf[pl.ds(c * rows, rows), :] - lam * x_ref[pl.ds(c * rows, rows), :]
        rf[pl.ds(c * rows, rows), :] = rr
        hb[2, 0, c] = rr[:cy].astype(BF16)
        hb[2, 1, c] = rr[cy:].astype(BF16)
    halo(2, "start")
    spread(rf, (W.at[2, v], L.at[1]))
    to_across(2).start()
    to_sib(2).start()

    halo(1, "wait_recv")

    @pl.loop(0, nc)
    def _(c):
        _, out = stencil(p_ref, c, 1)
        axf[pl.ds(c * rows, cy), :] = out[0]
        axf[pl.ds(c * rows + cy, cy), :] = out[1]

    spread(axf, (L.at[5],))
    to_across(0).wait_recv()
    relay(0).start()
    to_across(1).wait_recv()
    relay(1).start()

    halo(2, "wait_recv")

    @pl.loop(0, nc)
    def _(c):
        _, out = stencil(rf, c, 2)
        ar_ref[pl.ds(c * rows, cy), :] = out[0]
        ar_ref[pl.ds(c * rows + cy, cy), :] = out[1]

    spread(ar_ref, (L.at[4],))

    def gram(lo, hi):
        def body(k, acc):
            ch = pl.ds(pl.multiple_of(k * CH, CH), CH)
            a = L[:, :, ch].reshape(6 * nc, CH)
            b = W[lo:hi, :, :, ch].reshape((hi - lo) * 4 * nc, CH)
            return acc + lax.dot_general(a, b, (((1,), (1,)), ((), ())), preferred_element_type=F32)
        return lax.fori_loop(0, nl // CH, body, jnp.zeros((6 * nc, (hi - lo) * 4 * nc), F32))

    def rs_copy(e, d):
        dst = (t + d) % T
        return rc(gpart.at[e, dst], grs.at[e, d], rs_s.at[e, d], rs_r.at[e, d], dst, v)

    def rs_each(e, what):
        for d in range(1, T):
            @pl.when((t + d) % T < Q)
            def _():
                getattr(rs_copy(e, d), what)()

    def ag_copy(e, d, q):
        return rc(gout.at[e, q], gout.at[e, q], ag_s.at[e, d], ag_r.at[e, q], (t + d) % T, v)

    def reduce(e):
        @pl.when(t < Q)
        def _():
            total = gpart[e, t]
            for d in range(1, T):
                rc(gpart.at[e, 0], grs.at[e, d], rs_s.at[e, d], rs_r.at[e, d], (t + d) % T, v).wait_recv()
                total = total + grs[e, d]
            gout[e, t] = total * (1.0 / nvox)
            for d in range(1, T):
                ag_copy(e, d, t).start()

    to_sib(0).wait_recv()
    to_sib(1).wait_recv()
    relay(0).wait_recv()
    relay(1).wait_recv()
    gx = gram(0, 2)
    for q in range(Q):
        gpart[0, q] = gx[q * nc:(q + 1) * nc, :]
    rs_each(0, "start")

    to_across(2).wait_recv()
    relay(2).start()
    to_sib(2).wait_recv()
    reduce(0)
    relay(2).wait_recv()
    gr = gram(2, 3)
    pad = jnp.zeros((nc, 4 * nc), F32)
    for q in range(Q):
        gpart[1, q] = jnp.concatenate([gr[q * nc:(q + 1) * nc, :], pad], axis=1)
    rs_each(1, "start")

    ct = jnp.concatenate([ct_x, ct_p, ct_r], axis=1)

    @pl.loop(0, nl // CH)
    def _(k):
        ch = pl.ds(pl.multiple_of(k * CH, CH), CH)
        o = jnp.dot(ct, W[:, :, :, ch].reshape(12 * nc, CH), preferred_element_type=F32)
        for r in range(CH // cz):
            at = pl.ds(k * (CH // cz) + r, nc, stride=rows)
            xo_ref[at, :] = o[:nc, r * cz:(r + 1) * cz]
            po_ref[at, :] = o[nc:, r * cz:(r + 1) * cz]

    reduce(1)
    for e in range(2):
        for q in range(Q):
            @pl.when(t != q)
            def _():
                ag_copy(e, 1, q).wait_recv()
    n4 = 4 * nc
    for h in range(2):
        for a in range(3):
            q = 3 * h + a
            xp = gout[0, q]
            g_ref[h, a * nc:(a + 1) * nc, :] = jnp.concatenate(
                [xp[:, :n4], gout[1, q][:, :n4], xp[:, n4:]], axis=1)

    both(ig_left, ig_right, "wait_send")
    for f in range(3):
        halo(f, "wait_send")
        to_across(f).wait_send()
        to_sib(f).wait_send()
        relay(f).wait_send()
    for d in range(1, T):
        lam_copy(d).wait_send()
    for e in range(2):
        rs_each(e, "wait_send")

        @pl.when(t < Q)
        def _():
            for d in range(1, T):
                ag_copy(e, d, t).wait_send()


def shards(T, vectors, previous, intensity, counts, coef_x, coef_p):
    nc, cx, cy, cz = vectors.shape
    rows = cx * cy
    nl = rows * cz
    vm = pl.BlockSpec(memory_space=pltpu.VMEM)
    dma = pltpu.SemaphoreType.DMA
    xo, po, ar, g = pl.pallas_call(
        functools.partial(kernel, T, nc, cy, cz, nl * T),
        out_shape=[jax.ShapeDtypeStruct((nc * rows, cz), F32)] * 3 + [jax.ShapeDtypeStruct((2, 3 * nc, 12 * nc), F32)],
        in_specs=[vm, vm, vm, pl.BlockSpec(memory_space=pltpu.SMEM), vm, vm],
        out_specs=[vm] * 4,
        scratch_shapes=[
            pltpu.VMEM((2, 2, cy, cz), F32),
            pltpu.VMEM((2, 2, 2, cy, cz), F32),
            pltpu.VMEM((3, 2, nc, cy, cz), BF16),
            pltpu.VMEM((3, 2, nc, cy, cz), BF16),
            pltpu.VMEM((5, 3, cy, cz), F32),
            pltpu.VMEM((3, 4, nc, nl), BF16),
            pltpu.VMEM((6, nc, nl), BF16),
            pltpu.VMEM((nc * rows, cz), F32),
            pltpu.VMEM((nc * rows, cz), F32),
            pltpu.VMEM((128, cz), F32),
            pltpu.VMEM((T, 8, 128), F32),
            pltpu.VMEM((2, Q, nc, 8 * nc), F32),
            pltpu.VMEM((2, T, nc, 8 * nc), F32),
            pltpu.VMEM((2, Q, nc, 8 * nc), F32),
            dma((2,)), dma((2,)), dma((3, 2)), dma((3, 2)), dma((3, 3)), dma((3, 3)),
            dma((T,)), dma((T,)), dma((2, T)), dma((2, T)), dma((2, T)), dma((2, Q)),
        ],
        compiler_params=pltpu.CompilerParams(
            collective_id=0, has_side_effects=True, vmem_limit_bytes=40 * 1024 * 1024),
    )(vectors.reshape(nc * rows, cz), previous.reshape(nc * rows, cz), intensity, counts, coef_x, coef_p)
    shape = (nc, cx, cy, cz)
    return (
        xo.reshape(shape), po.reshape(shape), ar.reshape(shape),
        g[0].reshape(3, nc, 3, 4 * nc), g[1].reshape(3, nc, 3, 4 * nc),
    )


def solution(mesh):
    cols = P("vec", "tile", None, None)
    gram = P(None, "vec", None, None)
    return jax.shard_map(
        functools.partial(shards, mesh.shape["tile"]),
        mesh=mesh,
        in_specs=(cols, cols, P("tile", None, None), P("tile"), P(), P()),
        out_specs=(cols, cols, cols, gram, gram),
        check_vma=False,
    )
```

```python
import functools

import jax
import jax.numpy as jnp
from jax import lax
from jax.experimental import pallas as pl
from jax.experimental.pallas import tpu as pltpu
from jax.sharding import PartitionSpec as P

MESH = pl.DeviceIdType.MESH
F32 = jnp.float32
BF16 = jnp.bfloat16
Q = 6
CH = 1024


def kernel(
    T, nc, cy, cz, nvox,
    x_hbm, p_hbm, int_hbm, cnt_ref, cfx_hbm, cfp_hbm,
    xo_ref, po_ref, ar_ref, gs_ref, ga_ref,
    x_ref, p_ref, int_ref, cfx_ref, cfp_ref, in_s,
    igb, igh, hb, hh, coef, W, L, axf, apf, rf, lbuf, lamb, lamr,
    gpart, grs, gout,
    ig_s, ig_r, h_s, h_r, w_s, w_r, lam_s, lam_r, rs_s, rs_r, ag_s, ag_r,
):
    t = lax.axis_index("tile")
    v = lax.axis_index("vec")
    sib = v + 1 - 2 * (v % 2)
    across = (v + 2) % 4
    tl = (t + T - 1) % T
    tr = (t + 1) % T
    rows = 2 * cy
    nl = rows * cz

    def rc(src, dst, ss, rs, tile, vec):
        return pltpu.make_async_remote_copy(
            src_ref=src, dst_ref=dst, send_sem=ss, recv_sem=rs,
            device_id={"tile": tile, "vec": vec}, device_id_type=MESH)

    loads = [
        pltpu.make_async_copy(a, b, in_s.at[k])
        for k, (a, b) in enumerate((
            (x_hbm, x_ref), (int_hbm, int_ref), (p_hbm, p_ref), (cfx_hbm, cfx_ref), (cfp_hbm, cfp_ref)))
    ]
    barrier = pltpu.get_barrier_semaphore()
    for d in range(1, T):
        pl.semaphore_signal(barrier, inc=1, device_id={"tile": (t + d) % T, "vec": v}, device_id_type=MESH)
    pl.semaphore_signal(barrier, inc=1, device_id={"tile": t, "vec": sib}, device_id_type=MESH)
    pl.semaphore_signal(barrier, inc=1, device_id={"tile": t, "vec": across}, device_id_type=MESH)

    for load in loads:
        load.start()

    yy = lax.broadcasted_iota(jnp.int32, (cy, cz), 0)
    zz = lax.broadcasted_iota(jnp.int32, (cy, cz), 1)
    cnt = cnt_ref[0]
    loads[1].wait()
    for p in range(2):
        fg = jnp.where((p * cy + yy) * cz + zz < cnt, 1.0, 0.0).astype(F32)
        igb[p, 0] = int_ref[p]
        igb[p, 1] = fg * 0.9 + 0.1

    def to_halo(f, src):
        @pl.loop(0, nc, unroll=4)
        def _(c):
            for p in range(2):
                hb[f, p, c] = src[pl.ds(c * rows + p * cy, cy), :].astype(BF16)

    def spread(src, dsts):
        for r in range(rows):
            val = src[pl.ds(r, nc, stride=rows), :].astype(BF16)
            for dst in dsts:
                dst[:, r * cz:(r + 1) * cz] = val

    loads[0].wait()
    to_halo(0, x_ref)

    @pl.when(t == 0)
    def _():
        hh[0, 0] = jnp.zeros((nc, cy, cz), BF16)
        hh[1, 0] = jnp.zeros((nc, cy, cz), BF16)
        hh[2, 0] = jnp.zeros((nc, cy, cz), BF16)
        igh[0] = jnp.zeros((2, 2, cy, cz), F32)

    @pl.when(t == T - 1)
    def _():
        hh[0, 1] = jnp.zeros((nc, cy, cz), BF16)
        hh[1, 1] = jnp.zeros((nc, cy, cz), BF16)
        hh[2, 1] = jnp.zeros((nc, cy, cz), BF16)
        igh[1] = jnp.zeros((2, 2, cy, cz), F32)

    pl.semaphore_wait(barrier, T + 1)

    def ig_left():
        return rc(igb, igh.at[1], ig_s.at[0], ig_r.at[1], tl, v)

    def ig_right():
        return rc(igb, igh.at[0], ig_s.at[1], ig_r.at[0], tr, v)

    def h_left(f):
        return rc(hb.at[f, 0], hh.at[f, 1], h_s.at[f, 0], h_r.at[f, 1], tl, v)

    def h_right(f):
        return rc(hb.at[f, 1], hh.at[f, 0], h_s.at[f, 1], h_r.at[f, 0], tr, v)

    def both(left, right, what):
        @pl.when(t > 0)
        def _():
            c = right() if what == "wait_recv" else left()
            getattr(c, what)()

        @pl.when(t < T - 1)
        def _():
            c = left() if what == "wait_recv" else right()
            getattr(c, what)()

    def halo(f, what):
        both(lambda: h_left(f), lambda: h_right(f), what)

    def to_sib(f):
        return rc(W.at[f, v], W.at[f, v], w_s.at[f, 0], w_r.at[f, 0], t, sib)

    def to_across(f):
        return rc(W.at[f, v], W.at[f, v], w_s.at[f, 1], w_r.at[f, 1], t, across)

    def relay(f):
        return rc(W.at[f, across], W.at[f, across], w_s.at[f, 2], w_r.at[f, 2], t, sib)

    both(ig_left, ig_right, "start")
    halo(0, "start")
    loads[2].wait()
    to_halo(1, p_ref)
    spread(x_ref, (W.at[0, v], L.at[0]))
    to_across(0).start()
    to_sib(0).start()
    spread(p_ref, (W.at[1, v], L.at[2]))
    to_across(1).start()
    to_sib(1).start()
    loads[3].wait()
    loads[4].wait()

    pick = jnp.where(
        lax.broadcasted_iota(jnp.int32, (nc, 4 * nc), 1) == v * nc + lax.broadcasted_iota(jnp.int32, (nc, 4 * nc), 0),
        1.0, 0.0).astype(BF16)

    def own_t(m):
        return lax.dot_general(pick, m, (((1,), (1,)), ((), ())), preferred_element_type=F32)

    zero = jnp.zeros((nc, 4 * nc), F32)
    ct_x = jnp.concatenate([own_t(cfx_ref[0]), zero], axis=0).astype(BF16)
    ct_r = jnp.concatenate([own_t(cfx_ref[1]), own_t(cfp_ref[0])], axis=0).astype(BF16)
    ct_p = jnp.concatenate([own_t(cfx_ref[2]), own_t(cfp_ref[1])], axis=0).astype(BF16)

    both(ig_left, ig_right, "wait_recv")
    im = [igh[0, 0, 0], igh[0, 1, 0], igb[0, 0], igb[1, 0], igh[1, 0, 0], igh[1, 1, 0]]
    gg = [igh[0, 0, 1], igh[0, 1, 1], igb[0, 1], igb[1, 1], igh[1, 0, 1], igh[1, 1, 1]]

    def up(a, axis):
        return pltpu.roll(a, a.shape[axis] - 1, axis)

    def down(a, axis):
        return pltpu.roll(a, 1, axis)

    wx = [jnp.exp(-((im[k] - im[k + 1]) ** 2)) * gg[k] * gg[k + 1] for k in range(5)]
    wx[1] = jnp.where(t > 0, wx[1], 0.0)
    wx[3] = jnp.where(t < T - 1, wx[3], 0.0)
    wx[0] = jnp.where(t > 0, wx[0], 0.0)
    wx[4] = jnp.where(t < T - 1, wx[4], 0.0)
    inv, wys, wzs = {}, {}, {}
    for k in range(1, 5):
        wy = jnp.where(yy < cy - 1, jnp.exp(-((im[k] - up(im[k], 0)) ** 2)) * gg[k] * up(gg[k], 0), 0.0)
        wz = jnp.where(zz < cz - 1, jnp.exp(-((im[k] - up(im[k], 1)) ** 2)) * gg[k] * up(gg[k], 1), 0.0)
        deg = wx[k] + wx[k - 1] + wy + down(wy, 0) + wz + down(wz, 1)
        inv[k] = lax.rsqrt(deg)
        wys[k], wzs[k] = wy, wz
    cm = jnp.where(t > 0, inv[1] * wx[1] * inv[2], 0.0)
    c0 = inv[2] * wx[2] * inv[3]
    cp = jnp.where(t < T - 1, inv[3] * wx[3] * inv[4], 0.0)
    coef[0, 0] = cm
    coef[0, 1] = c0
    coef[0, 2] = cp
    for p in range(2):
        k = p + 2
        cyu = inv[k] * wys[k] * up(inv[k], 0)
        czu = inv[k] * wzs[k] * up(inv[k], 1)
        coef[1, p] = cyu
        coef[2, p] = down(cyu, 0)
        coef[3, p] = czu
        coef[4, p] = down(czu, 1)

    def inner(src, dst, c):
        fs = [src[pl.ds(c * rows, cy), :], src[pl.ds(c * rows + cy, cy), :]]
        for p in range(2):
            a = fs[p]
            s = coef[1, p] * up(a, 0) + coef[2, p] * down(a, 0)
            s = s + coef[3, p] * up(a, 1) + coef[4, p] * down(a, 1)
            s = s + coef[0, 1] * fs[1 - p]
            dst[pl.ds(c * rows + p * cy, cy), :] = a - s

    def outer(f, p, c):
        return coef[0, 2 * p] * hh[f, p, c].astype(F32)

    @pl.loop(0, nc, unroll=4)
    def _(c):
        inner(x_ref, axf, c)

    @pl.loop(0, nc, unroll=4)
    def _(c):
        inner(p_ref, apf, c)

    lbuf[...] = jnp.zeros_like(lbuf)

    halo(0, "wait_recv")

    @pl.loop(0, nc, unroll=4)
    def _(c):
        num, den = 0.0, 0.0
        for p in range(2):
            at = pl.ds(c * rows + p * cy, cy)
            ax = axf[at, :] - outer(0, p, c)
            axf[at, :] = ax
            hb[2, p, c] = ax.astype(BF16)
            num = num + ax * x_ref[at, :]
            den = den + x_ref[at, :] * x_ref[at, :]
        lbuf[pl.ds(c, 1), :] = jnp.sum(num, axis=0, keepdims=True)
        lbuf[pl.ds(nc + c, 1), :] = jnp.sum(den, axis=0, keepdims=True)

    halo(2, "start")
    lamb[0] = lax.dot_general(
        jnp.ones((8, cz), F32), lbuf[...], (((1,), (1,)), ((), ())),
        precision=lax.Precision.HIGHEST, preferred_element_type=F32)

    def lam_copy(d):
        return rc(lamb.at[0], lamb.at[d], lam_s.at[d], lam_r.at[d], (t + d) % T, v)

    for d in range(1, T):
        lam_copy(d).start()
    halo(1, "start")
    spread(axf, (L.at[3],))

    @pl.loop(0, nc, unroll=4)
    def _(c):
        inner(axf, ar_ref, c)

    for d in range(1, T):
        lam_copy(d).wait_recv()
    tot = lamb[0]
    for d in range(1, T):
        tot = tot + lamb[d]
    lams = tot / pltpu.roll(tot, 128 - nc, 1)

    for c in range(nc):
        lam = lams[0:1, c:c + 1]
        lamr[c] = jnp.broadcast_to(lam, (8, cz))
        at = pl.ds(c * rows, rows)
        rf[at, :] = axf[at, :] - lam * x_ref[at, :]
    spread(rf, (W.at[2, v], L.at[1]))
    to_across(2).start()
    to_sib(2).start()
    to_across(0).wait_recv()
    relay(0).start()
    to_across(1).wait_recv()
    relay(1).start()

    halo(2, "wait_recv")

    @pl.loop(0, nc, unroll=4)
    def _(c):
        for p in range(2):
            at = pl.ds(c * rows + p * cy, cy)
            ar_ref[at, :] = ar_ref[at, :] - outer(2, p, c) - lamr[c, 0:1, :] * axf[at, :]

    spread(ar_ref, (L.at[4],))

    halo(1, "wait_recv")

    @pl.loop(0, nc, unroll=4)
    def _(c):
        for p in range(2):
            at = pl.ds(c * rows + p * cy, cy)
            apf[at, :] = apf[at, :] - outer(1, p, c)

    spread(apf, (L.at[5],))

    def gram(lo, hi):
        def body(k, acc):
            ch = pl.ds(pl.multiple_of(k * CH, CH), CH)
            a = L[:, :, ch].reshape(6 * nc, CH)
            b = W[lo:hi, :, :, ch].reshape((hi - lo) * 4 * nc, CH)
            return acc + lax.dot_general(a, b, (((1,), (1,)), ((), ())), preferred_element_type=F32)
        return lax.fori_loop(0, nl // CH, body, jnp.zeros((6 * nc, (hi - lo) * 4 * nc), F32))

    def rs_copy(e, d):
        dst = (t + d) % T
        return rc(gpart.at[e, dst], grs.at[e, d], rs_s.at[e, d], rs_r.at[e, d], dst, v)

    def rs_each(e, what):
        for d in range(1, T):
            @pl.when((t + d) % T < Q)
            def _():
                getattr(rs_copy(e, d), what)()

    def ag_copy(e, d, q):
        return rc(gout.at[e, q], gout.at[e, q], ag_s.at[e, d], ag_r.at[e, q], (t + d) % T, v)

    def reduce(e):
        @pl.when(t < Q)
        def _():
            total = gpart[e, t].astype(F32)
            for d in range(1, T):
                rc(gpart.at[e, 0], grs.at[e, d], rs_s.at[e, d], rs_r.at[e, d], (t + d) % T, v).wait_recv()
                total = total + grs[e, d].astype(F32)
            gout[e, t] = (total * (1.0 / nvox)).astype(BF16)
            for d in range(1, T):
                ag_copy(e, d, t).start()

    to_sib(0).wait_recv()
    to_sib(1).wait_recv()
    relay(0).wait_recv()
    relay(1).wait_recv()
    gx = gram(0, 2)
    for q in range(Q):
        gpart[0, q] = gx[q * nc:(q + 1) * nc, :].astype(BF16)
    rs_each(0, "start")

    to_across(2).wait_recv()
    relay(2).start()
    to_sib(2).wait_recv()
    relay(2).wait_recv()
    gr = gram(2, 3)
    pad = jnp.zeros((nc, 4 * nc), F32)
    for q in range(Q):
        gpart[1, q] = jnp.concatenate([gr[q * nc:(q + 1) * nc, :], pad], axis=1).astype(BF16)
    rs_each(1, "start")

    ct = jnp.concatenate([ct_x, ct_p, ct_r], axis=1)

    def advance(k):
        ch = pl.ds(pl.multiple_of(k * CH, CH), CH)
        o = jnp.dot(ct, W[:, :, :, ch].reshape(12 * nc, CH), preferred_element_type=F32)
        for r in range(CH // cz):
            at = pl.ds(k * (CH // cz) + r, nc, stride=rows)
            xo_ref[at, :] = o[:nc, r * cz:(r + 1) * cz]
            po_ref[at, :] = o[nc:, r * cz:(r + 1) * cz]

    pl.loop(0, nl // CH // 2)(advance)
    reduce(0)
    reduce(1)
    pl.loop(nl // CH // 2, nl // CH)(advance)
    for e in range(2):
        for q in range(Q):
            @pl.when(t != q)
            def _():
                ag_copy(e, 1, q).wait_recv()
    n4 = 4 * nc
    for h, out in enumerate((gs_ref, ga_ref)):
        for a in range(3):
            xp = gout[0, 3 * h + a].astype(F32)
            out[a, 0] = xp[:, :n4]
            out[a, 1] = gout[1, 3 * h + a][:, :n4].astype(F32)
            out[a, 2] = xp[:, n4:]

    both(ig_left, ig_right, "wait_send")
    for f in range(3):
        halo(f, "wait_send")
        to_across(f).wait_send()
        to_sib(f).wait_send()
        relay(f).wait_send()
    for d in range(1, T):
        lam_copy(d).wait_send()
    for e in range(2):
        rs_each(e, "wait_send")

        @pl.when(t < Q)
        def _():
            for d in range(1, T):
                ag_copy(e, d, t).wait_send()


def shards(T, vectors, previous, intensity, counts, coef_x, coef_p):
    nc, cx, cy, cz = vectors.shape
    rows = cx * cy
    nl = rows * cz
    vm = pl.BlockSpec(memory_space=pltpu.VMEM)
    hbm = pl.BlockSpec(memory_space=pltpu.HBM)
    dma = pltpu.SemaphoreType.DMA
    xo, po, ar, gs, ga = pl.pallas_call(
        functools.partial(kernel, T, nc, cy, cz, nl * T),
        out_shape=[jax.ShapeDtypeStruct((nc * rows, cz), F32)] * 3 + [jax.ShapeDtypeStruct((3, 3, nc, 4 * nc), F32)] * 2,
        in_specs=[hbm, hbm, hbm, pl.BlockSpec(memory_space=pltpu.SMEM), hbm, hbm],
        out_specs=[vm] * 5,
        scratch_shapes=[
            pltpu.VMEM((nc * rows, cz), F32),
            pltpu.VMEM((nc * rows, cz), F32),
            pltpu.VMEM((cx, cy, cz), F32),
            pltpu.VMEM(coef_x.shape, BF16),
            pltpu.VMEM(coef_p.shape, BF16),
            dma((5,)),
            pltpu.VMEM((2, 2, cy, cz), F32),
            pltpu.VMEM((2, 2, 2, cy, cz), F32),
            pltpu.VMEM((3, 2, nc, cy, cz), BF16),
            pltpu.VMEM((3, 2, nc, cy, cz), BF16),
            pltpu.VMEM((5, 3, cy, cz), F32),
            pltpu.VMEM((3, 4, nc, nl), BF16),
            pltpu.VMEM((6, nc, nl), BF16),
            pltpu.VMEM((nc * rows, cz), F32),
            pltpu.VMEM((nc * rows, cz), F32),
            pltpu.VMEM((nc * rows, cz), F32),
            pltpu.VMEM((128, cz), F32),
            pltpu.VMEM((T, 8, 128), F32),
            pltpu.VMEM((nc, 8, cz), F32),
            pltpu.VMEM((2, Q, nc, 8 * nc), BF16),
            pltpu.VMEM((2, T, nc, 8 * nc), BF16),
            pltpu.VMEM((2, Q, nc, 8 * nc), BF16),
            dma((2,)), dma((2,)), dma((3, 2)), dma((3, 2)), dma((3, 3)), dma((3, 3)),
            dma((T,)), dma((T,)), dma((2, T)), dma((2, T)), dma((2, T)), dma((2, Q)),
        ],
        compiler_params=pltpu.CompilerParams(
            collective_id=0, has_side_effects=True, vmem_limit_bytes=62 * 1024 * 1024),
    )(vectors.reshape(nc * rows, cz), previous.reshape(nc * rows, cz), intensity, counts, coef_x, coef_p)
    shape = (nc, cx, cy, cz)
    return (
        xo.reshape(shape), po.reshape(shape), ar.reshape(shape),
        gs.transpose(0, 2, 1, 3), ga.transpose(0, 2, 1, 3),
    )


def solution(mesh):
    cols = P("vec", "tile", None, None)
    gram = P(None, "vec", None, None)
    return jax.shard_map(
        functools.partial(shards, mesh.shape["tile"]),
        mesh=mesh,
        in_specs=(cols, cols, P("tile", None, None), P("tile"), P(), P()),
        out_specs=(cols, cols, cols, gram, gram),
        check_vma=False,
    )
```

```python
import functools

import jax
import jax.numpy as jnp
from jax import lax
from jax.experimental import pallas as pl
from jax.experimental.pallas import tpu as pltpu
from jax.sharding import PartitionSpec as P

MESH = pl.DeviceIdType.MESH
F32 = jnp.float32
BF16 = jnp.bfloat16
Q = 6
CH = 1024


def kernel(
    T, nc, cy, cz, nvox,
    x_hbm, p_hbm, int_hbm, cnt_ref, cfx_hbm, cfp_hbm,
    xo_ref, po_ref, ar_ref, gs_ref, ga_ref,
    x_ref, p_ref, int_ref, cfx_ref, cfp_ref, in_s,
    igb, igh, hb, hh, coef, W, L, axf, apf, rf, lbuf, lamb, lamr,
    gpart, grs, gout,
    ig_s, ig_r, h_s, h_r, w_s, w_r, lam_s, lam_r, rs_s, rs_r, ag_s, ag_r,
):
    t = lax.axis_index("tile")
    v = lax.axis_index("vec")
    sib = v + 1 - 2 * (v % 2)
    across = (v + 2) % 4
    tl = (t + T - 1) % T
    tr = (t + 1) % T
    rows = 2 * cy
    nl = rows * cz

    def rc(src, dst, ss, rs, tile, vec):
        return pltpu.make_async_remote_copy(
            src_ref=src, dst_ref=dst, send_sem=ss, recv_sem=rs,
            device_id={"tile": tile, "vec": vec}, device_id_type=MESH)

    loads = [
        pltpu.make_async_copy(a, b, in_s.at[k])
        for k, (a, b) in enumerate((
            (x_hbm, x_ref), (int_hbm, int_ref), (p_hbm, p_ref), (cfx_hbm, cfx_ref), (cfp_hbm, cfp_ref)))
    ]
    barrier = pltpu.get_barrier_semaphore()
    for d in range(1, T):
        pl.semaphore_signal(barrier, inc=1, device_id={"tile": (t + d) % T, "vec": v}, device_id_type=MESH)
    pl.semaphore_signal(barrier, inc=1, device_id={"tile": t, "vec": sib}, device_id_type=MESH)
    pl.semaphore_signal(barrier, inc=1, device_id={"tile": t, "vec": across}, device_id_type=MESH)

    for load in loads:
        load.start()

    yy = lax.broadcasted_iota(jnp.int32, (cy, cz), 0)
    zz = lax.broadcasted_iota(jnp.int32, (cy, cz), 1)
    cnt = cnt_ref[0]
    loads[1].wait()
    for p in range(2):
        fg = jnp.where((p * cy + yy) * cz + zz < cnt, 1.0, 0.0).astype(F32)
        igb[p, 0] = int_ref[p]
        igb[p, 1] = fg * 0.9 + 0.1

    def to_halo(f, src):
        @pl.loop(0, nc, unroll=4)
        def _(c):
            for p in range(2):
                hb[f, p, c] = src[pl.ds(c * rows + p * cy, cy), :].astype(BF16)

    def spread(src, dsts):
        for r in range(rows):
            val = src[pl.ds(r, nc, stride=rows), :].astype(BF16)
            for dst in dsts:
                dst[:, r * cz:(r + 1) * cz] = val

    loads[0].wait()
    to_halo(0, x_ref)

    @pl.when(t == 0)
    def _():
        hh[0, 0] = jnp.zeros((nc, cy, cz), BF16)
        hh[1, 0] = jnp.zeros((nc, cy, cz), BF16)
        hh[2, 0] = jnp.zeros((nc, cy, cz), BF16)
        igh[0] = jnp.zeros((2, 2, cy, cz), F32)

    @pl.when(t == T - 1)
    def _():
        hh[0, 1] = jnp.zeros((nc, cy, cz), BF16)
        hh[1, 1] = jnp.zeros((nc, cy, cz), BF16)
        hh[2, 1] = jnp.zeros((nc, cy, cz), BF16)
        igh[1] = jnp.zeros((2, 2, cy, cz), F32)

    pl.semaphore_wait(barrier, T + 1)

    def ig_left():
        return rc(igb, igh.at[1], ig_s.at[0], ig_r.at[1], tl, v)

    def ig_right():
        return rc(igb, igh.at[0], ig_s.at[1], ig_r.at[0], tr, v)

    def h_left(f):
        return rc(hb.at[f, 0], hh.at[f, 1], h_s.at[f, 0], h_r.at[f, 1], tl, v)

    def h_right(f):
        return rc(hb.at[f, 1], hh.at[f, 0], h_s.at[f, 1], h_r.at[f, 0], tr, v)

    def both(left, right, what):
        @pl.when(t > 0)
        def _():
            c = right() if what == "wait_recv" else left()
            getattr(c, what)()

        @pl.when(t < T - 1)
        def _():
            c = left() if what == "wait_recv" else right()
            getattr(c, what)()

    def halo(f, what):
        both(lambda: h_left(f), lambda: h_right(f), what)

    def to_sib(f):
        return rc(W.at[f, v], W.at[f, v], w_s.at[f, 0], w_r.at[f, 0], t, sib)

    def to_across(f):
        return rc(W.at[f, v], W.at[f, v], w_s.at[f, 1], w_r.at[f, 1], t, across)

    def relay(f):
        return rc(W.at[f, across], W.at[f, across], w_s.at[f, 2], w_r.at[f, 2], t, sib)

    both(ig_left, ig_right, "start")
    halo(0, "start")
    loads[2].wait()
    to_halo(1, p_ref)
    spread(x_ref, (W.at[0, v], L.at[0]))
    to_across(0).start()
    to_sib(0).start()
    spread(p_ref, (W.at[1, v], L.at[2]))
    to_across(1).start()
    to_sib(1).start()
    loads[3].wait()
    loads[4].wait()

    pick = jnp.where(
        lax.broadcasted_iota(jnp.int32, (nc, 4 * nc), 1) == v * nc + lax.broadcasted_iota(jnp.int32, (nc, 4 * nc), 0),
        1.0, 0.0).astype(BF16)

    def own_t(m):
        return lax.dot_general(pick, m, (((1,), (1,)), ((), ())), preferred_element_type=F32)

    zero = jnp.zeros((nc, 4 * nc), F32)
    ct_x = jnp.concatenate([own_t(cfx_ref[0]), zero], axis=0).astype(BF16)
    ct_r = jnp.concatenate([own_t(cfx_ref[1]), own_t(cfp_ref[0])], axis=0).astype(BF16)
    ct_p = jnp.concatenate([own_t(cfx_ref[2]), own_t(cfp_ref[1])], axis=0).astype(BF16)

    both(ig_left, ig_right, "wait_recv")
    im = [igh[0, 0, 0], igh[0, 1, 0], igb[0, 0], igb[1, 0], igh[1, 0, 0], igh[1, 1, 0]]
    gg = [igh[0, 0, 1], igh[0, 1, 1], igb[0, 1], igb[1, 1], igh[1, 0, 1], igh[1, 1, 1]]

    def up(a, axis):
        return pltpu.roll(a, a.shape[axis] - 1, axis)

    def down(a, axis):
        return pltpu.roll(a, 1, axis)

    wx = [jnp.exp(-((im[k] - im[k + 1]) ** 2)) * gg[k] * gg[k + 1] for k in range(5)]
    wx[1] = jnp.where(t > 0, wx[1], 0.0)
    wx[3] = jnp.where(t < T - 1, wx[3], 0.0)
    wx[0] = jnp.where(t > 0, wx[0], 0.0)
    wx[4] = jnp.where(t < T - 1, wx[4], 0.0)
    inv, wys, wzs = {}, {}, {}
    for k in range(1, 5):
        wy = jnp.where(yy < cy - 1, jnp.exp(-((im[k] - up(im[k], 0)) ** 2)) * gg[k] * up(gg[k], 0), 0.0)
        wz = jnp.where(zz < cz - 1, jnp.exp(-((im[k] - up(im[k], 1)) ** 2)) * gg[k] * up(gg[k], 1), 0.0)
        deg = wx[k] + wx[k - 1] + wy + down(wy, 0) + wz + down(wz, 1)
        inv[k] = lax.rsqrt(deg)
        wys[k], wzs[k] = wy, wz
    cm = jnp.where(t > 0, inv[1] * wx[1] * inv[2], 0.0)
    c0 = inv[2] * wx[2] * inv[3]
    cp = jnp.where(t < T - 1, inv[3] * wx[3] * inv[4], 0.0)
    coef[0, 0] = cm
    coef[0, 1] = c0
    coef[0, 2] = cp
    for p in range(2):
        k = p + 2
        cyu = inv[k] * wys[k] * up(inv[k], 0)
        czu = inv[k] * wzs[k] * up(inv[k], 1)
        coef[1, p] = cyu
        coef[2, p] = down(cyu, 0)
        coef[3, p] = czu
        coef[4, p] = down(czu, 1)

    def inner(src, dst, c):
        fs = [src[pl.ds(c * rows, cy), :], src[pl.ds(c * rows + cy, cy), :]]
        for p in range(2):
            a = fs[p]
            s = coef[1, p] * up(a, 0) + coef[2, p] * down(a, 0)
            s = s + coef[3, p] * up(a, 1) + coef[4, p] * down(a, 1)
            s = s + coef[0, 1] * fs[1 - p]
            dst[pl.ds(c * rows + p * cy, cy), :] = a - s

    def outer(f, p, c):
        return coef[0, 2 * p] * hh[f, p, c].astype(F32)

    @pl.loop(0, nc, unroll=4)
    def _(c):
        inner(x_ref, axf, c)

    @pl.loop(0, nc, unroll=4)
    def _(c):
        inner(p_ref, apf, c)

    lbuf[...] = jnp.zeros_like(lbuf)

    halo(0, "wait_recv")

    @pl.loop(0, nc, unroll=4)
    def _(c):
        num, den = 0.0, 0.0
        for p in range(2):
            at = pl.ds(c * rows + p * cy, cy)
            ax = axf[at, :] - outer(0, p, c)
            axf[at, :] = ax
            hb[2, p, c] = ax.astype(BF16)
            num = num + ax * x_ref[at, :]
            den = den + x_ref[at, :] * x_ref[at, :]
        lbuf[pl.ds(c, 1), :] = jnp.sum(num, axis=0, keepdims=True)
        lbuf[pl.ds(nc + c, 1), :] = jnp.sum(den, axis=0, keepdims=True)

    halo(2, "start")
    lamb[0] = lax.dot_general(
        jnp.ones((8, cz), F32), lbuf[...], (((1,), (1,)), ((), ())),
        precision=lax.Precision.HIGHEST, preferred_element_type=F32)

    def lam_copy(d):
        return rc(lamb.at[0], lamb.at[d], lam_s.at[d], lam_r.at[d], (t + d) % T, v)

    for d in range(1, T):
        lam_copy(d).start()
    halo(1, "start")
    spread(axf, (L.at[3],))

    @pl.loop(0, nc, unroll=4)
    def _(c):
        inner(axf, ar_ref, c)

    for d in range(1, T):
        lam_copy(d).wait_recv()
    tot = lamb[0]
    for d in range(1, T):
        tot = tot + lamb[d]
    lams = tot / pltpu.roll(tot, 128 - nc, 1)

    for c in range(nc):
        lam = lams[0:1, c:c + 1]
        lamr[c] = jnp.broadcast_to(lam, (8, cz))
        at = pl.ds(c * rows, rows)
        rf[at, :] = axf[at, :] - lam * x_ref[at, :]
    spread(rf, (W.at[2, v], L.at[1]))
    to_across(2).start()
    to_sib(2).start()
    to_across(0).wait_recv()
    relay(0).start()
    to_across(1).wait_recv()
    relay(1).start()

    halo(2, "wait_recv")

    @pl.loop(0, nc, unroll=4)
    def _(c):
        for p in range(2):
            at = pl.ds(c * rows + p * cy, cy)
            ar_ref[at, :] = ar_ref[at, :] - outer(2, p, c) - lamr[c, 0:1, :] * axf[at, :]

    spread(ar_ref, (L.at[4],))

    halo(1, "wait_recv")

    @pl.loop(0, nc, unroll=4)
    def _(c):
        for p in range(2):
            at = pl.ds(c * rows + p * cy, cy)
            apf[at, :] = apf[at, :] - outer(1, p, c)

    spread(apf, (L.at[5],))

    def gram(lo, hi):
        def body(k, acc):
            ch = pl.ds(pl.multiple_of(k * CH, CH), CH)
            a = L[:, :, ch].reshape(6 * nc, CH)
            b = W[lo:hi, :, :, ch].reshape((hi - lo) * 4 * nc, CH)
            return acc + lax.dot_general(a, b, (((1,), (1,)), ((), ())), preferred_element_type=F32)
        return lax.fori_loop(0, nl // CH, body, jnp.zeros((6 * nc, (hi - lo) * 4 * nc), F32), unroll=True)

    def rs_copy(e, d):
        dst = (t + d) % T
        return rc(gpart.at[e, dst], grs.at[e, d], rs_s.at[e, d], rs_r.at[e, d], dst, v)

    def rs_each(e, what):
        for d in range(1, T):
            @pl.when((t + d) % T < Q)
            def _():
                getattr(rs_copy(e, d), what)()

    def ag_copy(e, d, q):
        return rc(gout.at[e, q], gout.at[e, q], ag_s.at[e, d], ag_r.at[e, q], (t + d) % T, v)

    def reduce(e):
        @pl.when(t < Q)
        def _():
            total = gpart[e, t]
            for d in range(1, T):
                rc(gpart.at[e, 0], grs.at[e, d], rs_s.at[e, d], rs_r.at[e, d], (t + d) % T, v).wait_recv()
                total = total + grs[e, d]
            gout[e, t] = (total * (1.0 / nvox)).astype(BF16)
            for d in range(1, T):
                ag_copy(e, d, t).start()

    to_sib(0).wait_recv()
    to_sib(1).wait_recv()
    relay(0).wait_recv()
    relay(1).wait_recv()
    gx = gram(0, 2)
    for q in range(Q):
        gpart[0, q] = gx[q * nc:(q + 1) * nc, :]
    rs_each(0, "start")

    to_across(2).wait_recv()
    relay(2).start()
    to_sib(2).wait_recv()
    relay(2).wait_recv()
    gr = gram(2, 3)
    pad = jnp.zeros((nc, 4 * nc), F32)
    for q in range(Q):
        gpart[1, q] = jnp.concatenate([gr[q * nc:(q + 1) * nc, :], pad], axis=1)
    rs_each(1, "start")

    ct = jnp.concatenate([ct_x, ct_p, ct_r], axis=1)

    def advance(k):
        ch = pl.ds(pl.multiple_of(k * CH, CH), CH)
        o = jnp.dot(ct, W[:, :, :, ch].reshape(12 * nc, CH), preferred_element_type=F32)
        for r in range(CH // cz):
            at = pl.ds(k * (CH // cz) + r, nc, stride=rows)
            xo_ref[at, :] = o[:nc, r * cz:(r + 1) * cz]
            po_ref[at, :] = o[nc:, r * cz:(r + 1) * cz]

    pl.loop(0, nl // CH // 2, unroll=2)(advance)
    reduce(0)
    reduce(1)
    pl.loop(nl // CH // 2, nl // CH, unroll=2)(advance)
    for e in range(2):
        for q in range(Q):
            @pl.when(t != q)
            def _():
                ag_copy(e, 1, q).wait_recv()
    n4 = 4 * nc
    for h, out in enumerate((gs_ref, ga_ref)):
        for a in range(3):
            xp = gout[0, 3 * h + a].astype(F32)
            out[a, 0] = xp[:, :n4]
            out[a, 1] = gout[1, 3 * h + a][:, :n4].astype(F32)
            out[a, 2] = xp[:, n4:]

    both(ig_left, ig_right, "wait_send")
    for f in range(3):
        halo(f, "wait_send")
        to_across(f).wait_send()
        to_sib(f).wait_send()
        relay(f).wait_send()
    for d in range(1, T):
        lam_copy(d).wait_send()
    for e in range(2):
        rs_each(e, "wait_send")

        @pl.when(t < Q)
        def _():
            for d in range(1, T):
                ag_copy(e, d, t).wait_send()


def shards(T, vectors, previous, intensity, counts, coef_x, coef_p):
    nc, cx, cy, cz = vectors.shape
    rows = cx * cy
    nl = rows * cz
    vm = pl.BlockSpec(memory_space=pltpu.VMEM)
    hbm = pl.BlockSpec(memory_space=pltpu.HBM)
    dma = pltpu.SemaphoreType.DMA
    xo, po, ar, gs, ga = pl.pallas_call(
        functools.partial(kernel, T, nc, cy, cz, nl * T),
        out_shape=[jax.ShapeDtypeStruct((nc * rows, cz), F32)] * 3 + [jax.ShapeDtypeStruct((3, 3, nc, 4 * nc), F32)] * 2,
        in_specs=[hbm, hbm, hbm, pl.BlockSpec(memory_space=pltpu.SMEM), hbm, hbm],
        out_specs=[vm] * 5,
        scratch_shapes=[
            pltpu.VMEM((nc * rows, cz), F32),
            pltpu.VMEM((nc * rows, cz), F32),
            pltpu.VMEM((cx, cy, cz), F32),
            pltpu.VMEM(coef_x.shape, BF16),
            pltpu.VMEM(coef_p.shape, BF16),
            dma((5,)),
            pltpu.VMEM((2, 2, cy, cz), F32),
            pltpu.VMEM((2, 2, 2, cy, cz), F32),
            pltpu.VMEM((3, 2, nc, cy, cz), BF16),
            pltpu.VMEM((3, 2, nc, cy, cz), BF16),
            pltpu.VMEM((5, 3, cy, cz), F32),
            pltpu.VMEM((3, 4, nc, nl), BF16),
            pltpu.VMEM((6, nc, nl), BF16),
            pltpu.VMEM((nc * rows, cz), F32),
            pltpu.VMEM((nc * rows, cz), F32),
            pltpu.VMEM((nc * rows, cz), F32),
            pltpu.VMEM((128, cz), F32),
            pltpu.VMEM((T, 8, 128), F32),
            pltpu.VMEM((nc, 8, cz), F32),
            pltpu.VMEM((2, Q, nc, 8 * nc), F32),
            pltpu.VMEM((2, T, nc, 8 * nc), F32),
            pltpu.VMEM((2, Q, nc, 8 * nc), BF16),
            dma((2,)), dma((2,)), dma((3, 2)), dma((3, 2)), dma((3, 3)), dma((3, 3)),
            dma((T,)), dma((T,)), dma((2, T)), dma((2, T)), dma((2, T)), dma((2, Q)),
        ],
        compiler_params=pltpu.CompilerParams(
            collective_id=0, has_side_effects=True, vmem_limit_bytes=52 * 1024 * 1024),
    )(vectors.reshape(nc * rows, cz), previous.reshape(nc * rows, cz), intensity, counts, coef_x, coef_p)
    shape = (nc, cx, cy, cz)
    return (
        xo.reshape(shape), po.reshape(shape), ar.reshape(shape),
        gs.transpose(0, 2, 1, 3), ga.transpose(0, 2, 1, 3),
    )


def solution(mesh):
    cols = P("vec", "tile", None, None)
    gram = P(None, "vec", None, None)
    return jax.shard_map(
        functools.partial(shards, mesh.shape["tile"]),
        mesh=mesh,
        in_specs=(cols, cols, P("tile", None, None), P("tile"), P(), P()),
        out_specs=(cols, cols, cols, gram, gram),
        check_vma=False,
    )
```
